32 devices in a mesh: groups: 2 (over x), gx: 16 (over z, y, core).
Axes of the slice: x: 2, y: 2, z: 4, core: 2. Of those that a mesh axis runs over, the one named last changes fastest.
Arguments:
- efield: float32 [3, 64, 64, 256], P(None, ('groups', 'gx')), parts along dimension 1, may hold values from -6 to 6
- hfield: float32 [3, 64, 64, 256], P(None, ('groups', 'gx')), parts along dimension 1, may hold values from -6 to 6
- material: int32 [64, 64, 256], P(('groups', 'gx')), parts along dimension 0, may hold values from 0 to 15
- mat_eps: float32 [16], replicated, may hold values from 1 to 4
- mat_sigma: float32 [16], replicated, may hold values from 0.05 to 1
- seg_owner: int32 [32768, 1], P(('groups', 'gx')), parts along dimension 0, may hold values from 0 to 15; in each aligned block of 1024 rows (0 to 1023, 1024 to 2047, ...) at most 128 rows name the same one
- seg_cell: int32 [32768], P(('groups', 'gx')), parts along dimension 0, may hold values from 0 to 32767
- chain_start: int32 [32768], P(('groups', 'gx')), parts along dimension 0, may hold values 0 or 1
- couple: float32 [3, 64, 32768], P(None, None, ('groups', 'gx')), parts along dimension 2, may hold values from -1.5 to 1.5
- voltage: float32 [64, 32768], P(None, ('groups', 'gx')), parts along dimension 1, may hold values from -6 to 6
- current: float32 [64, 32768], P(None, ('groups', 'gx')), parts along dimension 1, may hold values from -6 to 6
- induct_step: float32 [64, 64], replicated, may hold values from -0.04 to 0.8, as said below
- capac_step: float32 [64, 64], replicated, may hold values from -0.04 to 0.8, as said below
Outputs:
- efield_out: float32 [3, 64, 64, 256], P(None, ('groups', 'gx')), parts along dimension 1
- hfield_out: float32 [3, 64, 64, 256], P(None, ('groups', 'gx')), parts along dimension 1
- voltage_out: float32 [64, 32768], P(None, ('groups', 'gx')), parts along dimension 1
- current_out: float32 [64, 32768], P(None, ('groups', 'gx')), parts along dimension 1
The draws below stay inside these ranges and needn't reach their ends.
There are 2 independent parts, one for each index of `groups`. The reference program is written for one: setup_inputs(seed, part) draws one part's arguments, and reference() takes and returns one part's arrays. A program takes and returns all parts, laid end to end along the dimension named above; an argument that names none is the same for every part. Nothing has to cross between parts.
Inputs may be any that keep to these rules, and one draw needn't show every extreme that they name: `seg_owner`: among the 1024 segments of one device, at most 128 name the same device. `seg_cell`: Row-major index over the 2 x 64 x 256 cells of that device's slab. `induct_step`: Symmetric. `capac_step`: Symmetric.
All inputs are finite; a program needn't handle non-finite values. No bound on the sum of `chain_start` on one device may be relied on, other than what follows from the above.
Results may differ from the reference program's by a relative error of at most 0.0001.
Values sent between devices are 32-bit elements; how exact they have to be, the bound alone decides.
A program may use at most 128 MiB of HBM per device.

```python
import math
import jax
import jax.numpy as jnp
import numpy as np
from jax import lax

CX = 2
NY = 64
NZ = 256
SEG_DEV = 1024
NCOND = 64
NMAT = 16
STEPS = 4
NX = 32
NSEG = 16384
CAP = 128
N_GX = 16


def line_matrix(key, lower_bound, upper_bound):
    spread = jax.random.uniform(jax.random.fold_in(key, 1), (NCOND, NCOND), jnp.float32, -0.04, 0.04)
    middle = jax.random.uniform(jax.random.fold_in(key, 2), (NCOND,), jnp.float32, lower_bound, upper_bound)
    identity = jnp.eye(NCOND, dtype=jnp.float32)
    return 0.5 * (spread + spread.T) * (1.0 - identity) + identity * middle[None, :]


def draw_induct_step(key, part):
    key = jax.random.fold_in(key, 11)
    return line_matrix(key, 0.4, 0.8)


def draw_capac_step(key, part):
    key = jax.random.fold_in(key, 23)
    return line_matrix(key, 0.4, 0.8)


def place_ends(drawn, own_key, least, high):
    spot = [jax.random.randint(jax.random.fold_in(own_key, axis), (), 0, length) for axis, length in enumerate(drawn.shape)]
    main_axis = drawn.shape.index(max(drawn.shape))
    neighbour = spot[:main_axis] + [(spot[main_axis] + 1) % drawn.shape[main_axis]] + spot[main_axis + 1:]
    return drawn.at[tuple(spot)].set(least).at[tuple(neighbour)].set(high)


def level_of(stream_key, dims, split, low, largest):
    gain = 1.0
    for dim, blocks in split:
        draws = jax.random.uniform(jax.random.fold_in(jax.random.fold_in(stream_key, 6), dim), (blocks,), jnp.float32, low / len(split), largest / len(split))
        gain = gain * jnp.repeat(jnp.exp(draws), dims[dim] // blocks).reshape((-1,) + (1,) * (len(dims) - 1 - dim))
    return gain


def routed_block(stream_key, own, number, rows, number_of, top, reach, slope):
    order = jax.random.permutation(stream_key, number_of)
    heavy_load, usual = portions_of(number_of, rows * top, reach, slope, True), portions_of(number_of, rows * top, reach, slope, False)
    places = jnp.arange(number_of)

    def named(tallies, offset_by):
        used = int((tallies > 0).sum())
        fixed = max(1, used // 4)
        moved = fixed + (places - fixed + offset_by * (used - fixed)) % max(1, number_of - fixed)
        return jnp.zeros((number_of,), jnp.int32).at[order[jnp.where(places < fixed, places, moved)]].set(jnp.asarray(tallies, jnp.int32))

    tallies = jnp.where(number % 4 == 0, named(heavy_load, number // 4), named(usual, number - number // 4 - 1))
    mixed = jax.random.permutation(jax.random.fold_in(own, 3), number_of)
    giver, receiver = mixed[0:number_of // 2 * 2:2], mixed[1:number_of // 2 * 2:2]
    margin = jnp.minimum(tallies[giver] - 1, reach - tallies[receiver]) // 2
    margin = jnp.where((giver == order[0]) | (receiver == order[0]) | (tallies[receiver] == 0), 0, jnp.maximum(margin, 0))
    moved = jax.random.randint(jax.random.fold_in(own, 4), (number_of // 2,), 0, 1 << 20) % (margin + 1)
    tallies = tallies.at[giver].add(-moved).at[receiver].add(moved)
    labels = jnp.searchsorted(jnp.cumsum(tallies), jnp.arange(rows * top), side="right").astype(jnp.int32)
    table = labels.reshape(top, rows).T
    table = table[jax.random.permutation(jax.random.fold_in(own, 1), rows)]
    offset_by = jax.random.randint(jax.random.fold_in(own, 2), (rows, 1), 0, top)
    return jnp.take_along_axis(table, (jnp.arange(top)[None, :] + offset_by) % top, axis=1)


def portions_of(amount, total, limit, lean, full):
    weights = [(1 << 20) // math.isqrt(standing ** lean) + 1 for standing in range(1, amount + 1)]
    largest = limit if full else min(limit, max(-(-total // amount), total * weights[0] // sum(weights)))
    least = 1 if total - largest >= amount - 1 else 0
    holding, rest = [largest] + [least] * (amount - 1), total - largest - least * (amount - 1)
    while rest > 0:
        candidates = [i for i in range(1, amount) if holding[i] < largest] or [i for i in range(1, amount) if holding[i] < limit]
        mass, left = sum([weights[i] for i in candidates]), rest
        for i in candidates:
            more = min(limit - holding[i], max(1, left * weights[i] // mass), rest)
            holding[i] = holding[i] + more
            rest = rest - more
    return np.array(holding)


def noise(own_key, shape, deviation, most, shards=(), kind=jnp.bfloat16):
    values = deviation * jax.random.normal(own_key, shape, jnp.float32)
    if shards:
        values = values * level_of(own_key, shape, shards, -0.22, 0.18)
    return jnp.clip(values, -most, most).astype(kind)


def setup_inputs(seed: int = 0, part: int = 0) -> dict:
    key_of = jax.random.split(jax.random.key(seed), 14)
    part_keys = jax.random.split(jax.random.fold_in(key_of[13], part), 14)
    efield = noise(part_keys[0], (3, NX, NY, NZ), 1.0, 6.0, ((1, 16),), jnp.float32)
    hfield = noise(part_keys[1], (3, NX, NY, NZ), 1.0, 6.0, ((1, 16),), jnp.float32)
    material = place_ends(jax.random.randint(part_keys[2], (NX, NY, NZ), 0, NMAT), jax.random.fold_in(part_keys[2], 1), 0, NMAT - 1).astype(jnp.int32)
    mat_eps = jnp.clip(jnp.exp(jax.random.uniform(key_of[3], (NMAT,), jnp.float32, math.log(1.0), math.log(4.0))), 1.0, 4.0)
    mat_sigma = jnp.clip(jnp.exp(jax.random.uniform(key_of[4], (NMAT,), jnp.float32, math.log(0.05), math.log(1.0))), 0.05, 1.0)
    seg_owner_keys = jax.random.split(jax.random.fold_in(part_keys[5], 1), NSEG // SEG_DEV)
    seg_owner_turns = jax.random.permutation(jax.random.fold_in(part_keys[5], 3), NSEG // SEG_DEV)
    seg_owner = jax.vmap(lambda own, number: routed_block(jax.random.fold_in(part_keys[5], 2), own, number, SEG_DEV, N_GX, 1, CAP, 2))(seg_owner_keys, seg_owner_turns).reshape((NSEG, 1))
    seg_cell = place_ends(jax.random.randint(part_keys[6], (NSEG,), 0, CX * NY * NZ), jax.random.fold_in(part_keys[6], 1), 0, (CX * NY * NZ) - 1).astype(jnp.int32)
    chain_start = place_ends((jax.random.randint(part_keys[7], (NSEG,), 0, 64) < 1).astype(jnp.int32), jax.random.fold_in(part_keys[7], 1), 0, 1)
    couple = noise(part_keys[8], (3, NCOND, NSEG), 0.25, 1.5, ((2, 16),), jnp.float32)
    voltage = noise(part_keys[9], (NCOND, NSEG), 1.0, 6.0, ((1, 16),), jnp.float32)
    current = noise(part_keys[10], (NCOND, NSEG), 1.0, 6.0, ((1, 16),), jnp.float32)
    induct_step = draw_induct_step(jax.random.fold_in(key_of[13], 71), part)
    capac_step = draw_capac_step(jax.random.fold_in(key_of[13], 71), part)
    return {"efield": efield, "hfield": hfield, "material": material, "mat_eps": mat_eps, "mat_sigma": mat_sigma, "seg_owner": seg_owner, "seg_cell": seg_cell, "chain_start": chain_start, "couple": couple, "voltage": voltage, "current": current, "induct_step": induct_step, "capac_step": capac_step}


COURANT = 0.55


def forward_diff(values, dim_index):
    extent = values.shape[dim_index]
    widths = [(0, 0)] * values.ndim
    widths[dim_index] = (0, 1)
    padded = jnp.pad(values, widths)
    return lax.slice_in_dim(padded, 1, extent + 1, axis=dim_index) - values


def backward_diff(values, dim_index):
    extent = values.shape[dim_index]
    widths = [(0, 0)] * values.ndim
    widths[dim_index] = (1, 0)
    padded = jnp.pad(values, widths)
    return values - lax.slice_in_dim(padded, 0, extent, axis=dim_index)


def curl_forward(field):
    curl_x = forward_diff(field[2], 1) - forward_diff(field[1], 2)
    curl_y = forward_diff(field[0], 2) - forward_diff(field[2], 0)
    curl_z = forward_diff(field[1], 0) - forward_diff(field[0], 1)
    return jnp.stack([curl_x, curl_y, curl_z])


def curl_backward(field):
    curl_x = backward_diff(field[2], 1) - backward_diff(field[1], 2)
    curl_y = backward_diff(field[0], 2) - backward_diff(field[2], 0)
    curl_z = backward_diff(field[1], 0) - backward_diff(field[0], 1)
    return jnp.stack([curl_x, curl_y, curl_z])


def reference(efield, hfield, material, mat_eps, mat_sigma, seg_owner, seg_cell, chain_start, couple, voltage, current, induct_step, capac_step):
    loss_half = mat_sigma / (2.0 * mat_eps)
    keep_table = (1.0 - loss_half) / (1.0 + loss_half)
    drive_table = COURANT / (mat_eps * (1.0 + loss_half))
    keep_cell = keep_table[material]
    drive_cell = drive_table[material]
    cells_total = NX * NY * NZ
    global_cell = (seg_owner[:, 0] * (CX * NY * NZ) + seg_cell).astype(jnp.int32)
    start_float = chain_start.astype(jnp.float32)
    link_behind = 1.0 - start_float
    link_ahead = link_behind[1:]
    for step_index in range(STEPS):
        seen = efield.reshape(3, cells_total)[:, global_cell]
        hfield = hfield - COURANT * curl_forward(efield)
        source = couple[0] * seen[0][None] + couple[1] * seen[1][None] + couple[2] * seen[2][None]
        volt_next = jnp.concatenate([voltage[:, 1:] * link_ahead[None], jnp.zeros((NCOND, 1), jnp.float32)], axis=1)
        current = current - jnp.dot(induct_step, volt_next - voltage - source, precision=lax.Precision.HIGHEST, preferred_element_type=jnp.float32)
        seg_density = jnp.sum(couple * current[None], axis=1)
        density = jnp.zeros((3, cells_total), jnp.float32).at[:, global_cell].add(seg_density).reshape(efield.shape)
        curr_before = jnp.concatenate([jnp.zeros((NCOND, 1), jnp.float32), current[:, :-1]], axis=1) * link_behind[None]
        voltage = voltage - jnp.dot(capac_step, current - curr_before, precision=lax.Precision.HIGHEST, preferred_element_type=jnp.float32)
        efield = keep_cell * efield + drive_cell * (curl_backward(hfield) - density)
    return (efield, hfield, voltage, current)
```

```python
import functools

import jax
import jax.numpy as jnp
from jax import lax
from jax.experimental import pallas as pl
from jax.experimental.pallas import tpu as pltpu
from jax.sharding import PartitionSpec as P

STEPS = 4
COURANT = 0.55
MESH = pl.DeviceIdType.MESH
F32 = jnp.float32
BF16 = jnp.bfloat16
PAIRS = ((0, 0), (0, 1), (0, 2), (1, 1), (1, 2), (2, 2))
LANES = 128


def split(x):
    high = x.astype(BF16)
    return high, (x - high.astype(F32)).astype(BF16)


def dot(a, b):
    return jnp.dot(a, b, preferred_element_type=F32)


def dot_nt(a, b):
    return lax.dot_general(a, b, (((1,), (1,)), ((), ())), preferred_element_type=F32)


def iota(shape, dim):
    return lax.broadcasted_iota(jnp.int32, shape, dim)


def kernel(
    n,
    ny,
    e_in,
    h_in,
    material,
    mat_eps,
    mat_sigma,
    seg_owner,
    seg_cell,
    chain_start,
    couple,
    v_in,
    i_in,
    induct,
    capac,
    e_ref,
    h_ref,
    v_ref,
    i_ref,
    keep_ref,
    drive_ref,
    memb_ref,
    rank_ref,
    lc_ref,
    j_ref,
    ohz_ref,
    ohr_ref,
    spread_ref,
    m_ref,
    eg_ref,
    bout_ref,
    msg_out,
    msg_in,
    e_halo,
    h_halo,
    v_out,
    v_edge,
    i_out,
    i_edge,
    msg_ssem,
    msg_rsem,
    e_ssem,
    e_rsem,
    h_ssem,
    h_rsem,
    v_ssem,
    v_rsem,
    i_ssem,
    i_rsem,
):
    me = lax.axis_index("gx")
    _, rows, nz = e_in.shape
    cond, seg = v_in.shape
    cap = msg_in.shape[-1]
    slots = n * cap
    first, last = me == 0, me == n - 1
    not_first, not_last = me > 0, me < n - 1

    def partner(k):
        result, bit = 0, 1
        while bit < n:
            digit = (me // bit) % 2
            result = result + (((1 - digit) if (k & bit) else digit) * bit)
            bit *= 2
        return result

    partners = [partner(k) for k in range(n)]

    barrier = pltpu.get_barrier_semaphore()
    for k in range(1, n):
        pl.semaphore_signal(barrier, inc=1, device_id={"gx": partners[k]}, device_id_type=MESH)

    def to_partner(index, k):
        return pltpu.make_async_remote_copy(
            src_ref=msg_out.at[index, k],
            dst_ref=msg_in.at[index, k],
            send_sem=msg_ssem.at[index],
            recv_sem=msg_rsem.at[index],
            device_id={"gx": partners[k]},
            device_id_type=MESH,
        )

    def send_messages(index):
        for k in range(1, n):
            to_partner(index, k).start()
        msg_in[index, 0] = msg_out[index, 0]

    def wait_messages(index):
        part = msg_in.at[index, pl.ds(1, n - 1)]
        pltpu.make_async_copy(part, part, msg_rsem.at[index]).wait()

    def wait_sent(index):
        part = msg_out.at[index, pl.ds(1, n - 1)]
        pltpu.make_async_copy(part, part, msg_ssem.at[index]).wait()

    def to_neighbour(source, target, ssem, rsem, step, direction):
        return pltpu.make_async_remote_copy(
            src_ref=source,
            dst_ref=target.at[step],
            send_sem=ssem.at[step],
            recv_sem=rsem.at[step],
            device_id={"gx": (me + direction + n) % n},
            device_id_type=MESH,
        )

    def e_copy(source, step):
        return to_neighbour(
            source.at[pl.ds(1, 2), pl.ds(0, ny)], e_halo, e_ssem, e_rsem, step, -1
        )

    def h_copy(step):
        return to_neighbour(
            h_ref.at[pl.ds(1, 2), pl.ds(rows - ny, ny)], h_halo, h_ssem, h_rsem, step, 1
        )

    def v_copy(step):
        return to_neighbour(v_out.at[step], v_edge, v_ssem, v_rsem, step, -1)

    def i_copy(step):
        return to_neighbour(i_out.at[step], i_edge, i_ssem, i_rsem, step, 1)

    link_behind = 1.0 - chain_start[...].astype(F32)
    eye = iota((cond, v_edge.shape[-1]), 0) == iota((cond, v_edge.shape[-1]), 1)
    seg_lane = iota((1, seg), 1)

    def pack_edge(column):
        row = jnp.sum(jnp.where(eye, column, 0.0), axis=0, keepdims=True)
        return jnp.broadcast_to(row, (8, row.shape[1]))

    def unpack_edge(block):
        return jnp.sum(jnp.where(eye, block[0:1], 0.0), axis=1, keepdims=True)

    def times(matrix, x):
        mh, ml = split(matrix)
        xh, xl = split(x)
        return dot(mh, xh) + dot(mh, xl) + dot(ml, xh)

    def to_slots(values):
        product = jnp.concatenate([values] * n, axis=0) * memb_ref[...]
        high, low = split(product)
        result = dot_nt(high, rank_ref[...]) + dot_nt(low, rank_ref[...])
        return result.reshape(n, 8, cap)

    def from_slots(block):
        high, low = split(block.reshape(n * 8, cap))
        spread = dot(high, rank_ref[...]) + dot(low, rank_ref[...])
        return jnp.sum((spread * memb_ref[...]).reshape(n, 8, seg), axis=0)

    def as_rows(index):
        return jnp.concatenate([msg_in[index, k] for k in range(n)], axis=1)

    def send_volt(volt, step):
        v_out[step] = pack_edge(volt[:, 0:1] * link_behind[:, 0:1])

        @pl.when(not_first)
        def _():
            v_copy(step).start()

    def pending_current(current, volt, step):
        @pl.when(not_last)
        def _():
            v_copy(step).wait_recv()

        edge = unpack_edge(v_edge[step])
        ahead = pltpu.roll(volt * link_behind, seg - 1, 1)
        ahead = jnp.where(seg_lane == seg - 1, edge, ahead)
        pending = current - times(induct[...], ahead - volt)
        j_ref[...] = pending
        values = [jnp.sum(couple[c] * pending, axis=0, keepdims=True) for c in range(3)]
        zeros = jnp.zeros((1, seg), F32)
        bout_ref[...] = to_slots(jnp.concatenate([zeros] * 3 + values + [zeros] * 2, axis=0))

    row_of = iota((rows, 1), 0)
    y_of = row_of % ny
    z_of = iota((1, nz), 1)

    def ahead_y(x):
        return jnp.where(y_of == ny - 1, 0.0, pltpu.roll(x, rows - 1, 0))

    def ahead_z(x):
        return jnp.where(z_of == nz - 1, 0.0, pltpu.roll(x, nz - 1, 1))

    def behind_y(x):
        return jnp.where(y_of == 0, 0.0, pltpu.roll(x, 1, 0))

    def behind_z(x):
        return jnp.where(z_of == 0, 0.0, pltpu.roll(x, 1, 1))

    def magnetic(efield, hfield, step):
        @pl.when(not_last)
        def _():
            e_copy(e_in, step).wait_recv()

        if step > 0:

            @pl.when(not_last)
            def _():
                h_copy(step - 1).wait_send()

        ex, ey, ez = efield[0], efield[1], efield[2]
        next_y = jnp.concatenate([ey[ny:], e_halo[step, 0]], axis=0)
        next_z = jnp.concatenate([ez[ny:], e_halo[step, 1]], axis=0)
        h_ref[1] = hfield[1] - COURANT * ((ahead_z(ex) - ex) - (next_z - ez))
        h_ref[2] = hfield[2] - COURANT * ((next_y - ey) - (ahead_y(ex) - ex))

        @pl.when(not_last)
        def _():
            h_copy(step).start()

        h_ref[0] = hfield[0] - COURANT * ((ahead_y(ez) - ez) - (ahead_z(ey) - ey))

    def electric(efield, density, step):
        @pl.when(not_first)
        def _():
            h_copy(step).wait_recv()
            e_copy(e_in, step).wait_send()

        hx, hy, hz = h_ref[0], h_ref[1], h_ref[2]
        prev_y = jnp.concatenate([h_halo[step, 0], hy[: rows - ny]], axis=0)
        prev_z = jnp.concatenate([h_halo[step, 1], hz[: rows - ny]], axis=0)
        keep, drive = keep_ref[...], drive_ref[...]
        ex, ey, ez = efield[0], efield[1], efield[2]
        curl_y = (hx - behind_z(hx)) - (hz - prev_z)
        e_ref[1] = keep * ey + drive * (curl_y - density[1])
        curl_z = (hy - prev_y) - (hx - behind_y(hx))
        e_ref[2] = keep * ez + drive * (curl_z - density[2])
        if step + 1 < STEPS:

            @pl.when(not_first)
            def _():
                e_copy(e_ref, step + 1).start()

        curl_x = (hz - behind_y(hz)) - (hy - behind_z(hy))
        e_ref[0] = keep * ex + drive * (curl_x - density[0])

    chunk = 512

    def gather_cells(efield):
        high, low = split(efield.reshape(3 * rows, nz))
        for start in range(0, slots, chunk):
            part = pl.ds(start, chunk)
            onehot = ohz_ref[:, part]
            picked = dot(high, onehot) + dot(low, onehot)
            mask = ohr_ref[:, part].astype(F32)
            for c in range(3):
                eg_ref[c : c + 1, part] = jnp.sum(
                    picked[c * rows : (c + 1) * rows] * mask, axis=0, keepdims=True
                )

    def scatter_density(index):
        b = as_rows(index)
        e = [eg_ref[c : c + 1, :] for c in range(3)]
        m = [m_ref[i : i + 1, :] for i in range(6)]
        values = (
            b[3:4] + m[0] * e[0] + m[1] * e[1] + m[2] * e[2],
            b[4:5] + m[1] * e[0] + m[3] * e[1] + m[4] * e[2],
            b[5:6] + m[2] * e[0] + m[4] * e[1] + m[5] * e[2],
        )
        for c in range(3):
            high = values[c].astype(BF16).astype(F32)
            for i, value in enumerate((high, values[c] - high)):
                tile = jnp.broadcast_to(value, (16, slots)).astype(BF16)
                place = (i * 3 + c) * rows
                spread_ref[place : place + rows, :] = ohr_ref[...] * jnp.concatenate(
                    [tile] * (rows // 16), axis=0
                )
        total = dot_nt(spread_ref[...], ohz_ref[...])
        total = total[: 3 * rows] + total[3 * rows :]
        return [total[c * rows : (c + 1) * rows] for c in range(3)]

    def start_messages(step):
        for k in range(n):
            msg_out[2 + step, k] = bout_ref[k] + eg_ref[:, k * cap : (k + 1) * cap]
        send_messages(2 + step)

    relative = jnp.bitwise_xor(seg_owner[...], me)
    member = (iota((n, seg), 0) == relative).astype(F32)
    block = min(seg, 256)
    before = (iota((block, block), 0) < iota((block, block), 1)).astype(F32).astype(BF16)
    ahead_count = jnp.zeros((n, 1), F32)
    ranks = []
    for start in range(0, seg, block):
        part = member[:, start : start + block]
        count = dot(part.astype(BF16), before) + ahead_count
        ranks.append(jnp.sum(count * part, axis=0, keepdims=True))
        ahead_count = ahead_count + jnp.sum(part, axis=1, keepdims=True)
    rank = jnp.concatenate(ranks, axis=1).astype(jnp.int32)
    rank_ref[...] = (iota((cap, seg), 0) == rank).astype(F32).astype(BF16)
    memb_ref[...] = (iota((n * 8, seg), 0) // 8 == relative).astype(F32)
    cell = seg_cell[...]
    cell_row = (cell // nz).astype(F32)
    cell_z = (cell % nz).astype(F32)
    msg_out[0] = to_slots(
        jnp.concatenate([cell_row, cell_z, jnp.zeros((6, seg), F32)], axis=0)
    )

    pl.semaphore_wait(barrier, n - 1)

    send_messages(0)

    @pl.when(not_first)
    def _():
        e_copy(e_in, 0).start()

    send_volt(v_in[...], 0)

    @pl.when(last)
    def _():
        e_halo[...] = jnp.zeros_like(e_halo)
        v_edge[...] = jnp.zeros_like(v_edge)

    @pl.when(first)
    def _():
        h_halo[...] = jnp.zeros_like(h_halo)
        i_edge[...] = jnp.zeros_like(i_edge)

    eg_ref[...] = jnp.zeros_like(eg_ref)

    for c in range(3):
        lc_ref[c] = times(induct[...], couple[c])
    quad = [jnp.sum(couple[a] * lc_ref[b], axis=0, keepdims=True) for a, b in PAIRS]
    msg_out[1] = to_slots(jnp.concatenate(quad + [jnp.zeros((2, seg), F32)], axis=0))
    send_messages(1)

    pending_current(i_in[...], v_in[...], 0)

    loss = mat_sigma[...] / (2.0 * mat_eps[...])
    keep_table = (1.0 - loss) / (1.0 + loss)
    drive_table = COURANT / (mat_eps[...] * (1.0 + loss))
    keep = jnp.zeros((rows, nz), F32)
    drive = jnp.zeros((rows, nz), F32)
    for i in range(mat_eps.shape[1]):
        here = material[...] == i
        keep = jnp.where(here, keep_table[:, i : i + 1], keep)
        drive = jnp.where(here, drive_table[:, i : i + 1], drive)
    keep_ref[...] = keep
    drive_ref[...] = drive

    wait_messages(0)
    cells = as_rows(0).astype(jnp.int32)
    ohr_ref[...] = (iota((rows, slots), 0) == cells[0:1]).astype(F32).astype(BF16)
    ohz_ref[...] = (iota((nz, slots), 0) == cells[1:2]).astype(F32).astype(BF16)

    gather_cells(e_in[...])
    start_messages(0)
    magnetic(e_in[...], h_in[...], 0)
    wait_messages(1)
    m_ref[...] = as_rows(1)

    for step in range(STEPS):
        wait_messages(2 + step)
        seen = from_slots(msg_in[2 + step])
        current = (
            j_ref[...]
            + lc_ref[0] * seen[0:1]
            + lc_ref[1] * seen[1:2]
            + lc_ref[2] * seen[2:3]
        )
        i_ref[...] = current
        i_out[step] = pack_edge(current[:, seg - 1 : seg])

        @pl.when(not_last)
        def _():
            i_copy(step).start()

        density = scatter_density(2 + step)

        @pl.when(not_first)
        def _():
            i_copy(step).wait_recv()

        volt = v_in[...] if step == 0 else v_ref[...]
        current = i_ref[...]
        edge = unpack_edge(i_edge[step])
        behind = jnp.where(seg_lane == 0, edge, pltpu.roll(current, 1, 1)) * link_behind
        volt = volt - times(capac[...], current - behind)
        v_ref[...] = volt
        if step + 1 < STEPS:
            send_volt(volt, step + 1)
        electric(e_in[...] if step == 0 else e_ref[...], density, step)
        if step + 1 < STEPS:
            gather_cells(e_ref[...])
            pending_current(i_ref[...], v_ref[...], step + 1)
            start_messages(step + 1)
            magnetic(e_ref[...], h_ref[...], step + 1)

    for index in range(STEPS + 2):
        wait_sent(index)

    @pl.when(not_last)
    def _():
        h_copy(STEPS - 1).wait_send()
        for step in range(STEPS):
            i_copy(step).wait_send()

    @pl.when(not_first)
    def _():
        for step in range(STEPS):
            v_copy(step).wait_send()


def per_device(
    n,
    efield,
    hfield,
    material,
    mat_eps,
    mat_sigma,
    seg_owner,
    seg_cell,
    chain_start,
    couple,
    voltage,
    current,
    induct_step,
    capac_step,
):
    _, nx, ny, nz = efield.shape
    rows = nx * ny
    cond, seg = voltage.shape
    cap = -(-(2 * seg // n) // LANES) * LANES
    edge = -(-cond // LANES) * LANES
    slots = n * cap
    dma = pltpu.SemaphoreType.DMA
    scratch = [
        pltpu.VMEM((rows, nz), F32),
        pltpu.VMEM((rows, nz), F32),
        pltpu.VMEM((n * 8, seg), F32),
        pltpu.VMEM((cap, seg), BF16),
        pltpu.VMEM((3, cond, seg), F32),
        pltpu.VMEM((cond, seg), F32),
        pltpu.VMEM((nz, slots), BF16),
        pltpu.VMEM((rows, slots), BF16),
        pltpu.VMEM((6 * rows, slots), BF16),
        pltpu.VMEM((8, slots), F32),
        pltpu.VMEM((8, slots), F32),
        pltpu.VMEM((n, 8, cap), F32),
        pltpu.VMEM((STEPS + 2, n, 8, cap), F32),
        pltpu.VMEM((STEPS + 2, n, 8, cap), F32),
        pltpu.VMEM((STEPS, 2, ny, nz), F32),
        pltpu.VMEM((STEPS, 2, ny, nz), F32),
        pltpu.VMEM((STEPS, 8, edge), F32),
        pltpu.VMEM((STEPS, 8, edge), F32),
        pltpu.VMEM((STEPS, 8, edge), F32),
        pltpu.VMEM((STEPS, 8, edge), F32),
        dma((STEPS + 2,)),
        dma((STEPS + 2,)),
    ] + [dma((STEPS,))] * 8
    vmem = pl.BlockSpec(memory_space=pltpu.VMEM)
    out = pl.pallas_call(
        functools.partial(kernel, n, ny),
        out_shape=(
            jax.ShapeDtypeStruct((3, rows, nz), F32),
            jax.ShapeDtypeStruct((3, rows, nz), F32),
            jax.ShapeDtypeStruct((cond, seg), F32),
            jax.ShapeDtypeStruct((cond, seg), F32),
        ),
        in_specs=[vmem] * 13,
        out_specs=(vmem,) * 4,
        scratch_shapes=scratch,
        compiler_params=pltpu.CompilerParams(
            collective_id=0, has_side_effects=True, vmem_limit_bytes=48 * 1024 * 1024
        ),
        name="leapfrog",
    )(
        efield.reshape(3, rows, nz),
        hfield.reshape(3, rows, nz),
        material.reshape(rows, nz),
        mat_eps.reshape(1, -1),
        mat_sigma.reshape(1, -1),
        seg_owner.reshape(1, seg),
        seg_cell.reshape(1, seg),
        chain_start.reshape(1, seg),
        couple,
        voltage,
        current,
        induct_step,
        capac_step,
    )
    return (
        out[0].reshape(efield.shape),
        out[1].reshape(hfield.shape),
        out[2],
        out[3],
    )


def solution(mesh):
    placed = (
        P(None, ("groups", "gx"), None, None),
        P(None, ("groups", "gx"), None, None),
        P(("groups", "gx"), None, None),
        P(),
        P(),
        P(("groups", "gx"), None),
        P(("groups", "gx")),
        P(("groups", "gx")),
        P(None, None, ("groups", "gx")),
        P(None, ("groups", "gx")),
        P(None, ("groups", "gx")),
        P(),
        P(),
    )
    return jax.shard_map(
        functools.partial(per_device, mesh.shape["gx"]),
        mesh=mesh,
        in_specs=placed,
        out_specs=(
            P(None, ("groups", "gx"), None, None),
            P(None, ("groups", "gx"), None, None),
            P(None, ("groups", "gx")),
            P(None, ("groups", "gx")),
        ),
        check_vma=False,
    )
```

```python
import functools

import jax
import jax.numpy as jnp
from jax import lax
from jax.experimental import pallas as pl
from jax.experimental.pallas import tpu as pltpu
from jax.sharding import PartitionSpec as P

STEPS = 4
COURANT = 0.55
MESH = pl.DeviceIdType.MESH
F32 = jnp.float32
BF16 = jnp.bfloat16
PAIRS = ((0, 0), (0, 1), (0, 2), (1, 1), (1, 2), (2, 2))
LANES = 128


def split(x):
    high = x.astype(BF16)
    return high, (x - high.astype(F32)).astype(BF16)


def dot(a, b):
    return jnp.dot(a, b, preferred_element_type=F32)


def dot_nt(a, b):
    return lax.dot_general(a, b, (((1,), (1,)), ((), ())), preferred_element_type=F32)


def iota(shape, dim):
    return lax.broadcasted_iota(jnp.int32, shape, dim)


def kernel(
    n,
    ny,
    *refs,
):
    sources, refs = refs[:13], refs[13:]
    (
        e_ref,
        h_ref,
        v_ref,
        i_ref,
        material,
        mat_eps,
        mat_sigma,
        seg_owner,
        seg_cell,
        chain_start,
        couple,
        induct,
        capac,
        load_sem,
        keep_ref,
        drive_ref,
        memb_ref,
        rank_ref,
        lc_ref,
        j_ref,
        ohz_ref,
        ohr_ref,
        spread_ref,
        m_ref,
        eg_ref,
        bout_ref,
        msg_out,
        msg_in,
        e_halo,
        h_halo,
        v_out,
        v_edge,
        i_out,
        i_edge,
        msg_ssem,
        msg_rsem,
        e_ssem,
        e_rsem,
        h_ssem,
        h_rsem,
        v_ssem,
        v_rsem,
        i_ssem,
        i_rsem,
    ) = refs
    me = lax.axis_index("gx")
    _, rows, nz = e_ref.shape
    cond, seg = v_ref.shape
    cap = msg_in.shape[-1]
    slots = n * cap
    first, last = me == 0, me == n - 1
    not_first, not_last = me > 0, me < n - 1

    def partner(k):
        result, bit = 0, 1
        while bit < n:
            digit = (me // bit) % 2
            result = result + (((1 - digit) if (k & bit) else digit) * bit)
            bit *= 2
        return result

    partners = [partner(k) for k in range(n)]

    places = {
        "seg_owner": (5, seg_owner),
        "seg_cell": (6, seg_cell),
        "efield": (0, e_ref),
        "chain_start": (7, chain_start),
        "voltage": (9, v_ref),
        "induct": (11, induct),
        "couple": (8, couple),
        "current": (10, i_ref),
        "mat_eps": (3, mat_eps),
        "mat_sigma": (4, mat_sigma),
        "material": (2, material),
        "hfield": (1, h_ref),
        "capac": (12, capac),
    }

    def load(name):
        index, target = places[name]
        return pltpu.make_async_copy(sources[index], target, load_sem.at[index])

    for name in places:
        load(name).start()

    barrier = pltpu.get_barrier_semaphore()
    for k in range(1, n):
        pl.semaphore_signal(barrier, inc=1, device_id={"gx": partners[k]}, device_id_type=MESH)

    def to_partner(index, k):
        return pltpu.make_async_remote_copy(
            src_ref=msg_out.at[index, k],
            dst_ref=msg_in.at[index, k],
            send_sem=msg_ssem.at[index],
            recv_sem=msg_rsem.at[index],
            device_id={"gx": partners[k]},
            device_id_type=MESH,
        )

    def send_messages(index):
        for k in range(1, n):
            to_partner(index, k).start()
        msg_in[index, 0] = msg_out[index, 0]

    def wait_messages(index):
        part = msg_in.at[index, pl.ds(1, n - 1)]
        pltpu.make_async_copy(part, part, msg_rsem.at[index]).wait()

    def wait_sent(index):
        part = msg_out.at[index, pl.ds(1, n - 1)]
        pltpu.make_async_copy(part, part, msg_ssem.at[index]).wait()

    def to_neighbour(source, target, ssem, rsem, step, direction):
        return pltpu.make_async_remote_copy(
            src_ref=source,
            dst_ref=target.at[step],
            send_sem=ssem.at[step],
            recv_sem=rsem.at[step],
            device_id={"gx": (me + direction + n) % n},
            device_id_type=MESH,
        )

    def e_copy(step):
        return to_neighbour(
            e_ref.at[pl.ds(1, 2), pl.ds(0, ny)], e_halo, e_ssem, e_rsem, step, -1
        )

    def h_copy(step):
        return to_neighbour(
            h_ref.at[pl.ds(1, 2), pl.ds(rows - ny, ny)], h_halo, h_ssem, h_rsem, step, 1
        )

    def v_copy(step):
        return to_neighbour(v_out.at[step], v_edge, v_ssem, v_rsem, step, -1)

    def i_copy(step):
        return to_neighbour(i_out.at[step], i_edge, i_ssem, i_rsem, step, 1)

    load("seg_owner").wait()
    load("seg_cell").wait()
    relative = jnp.bitwise_xor(seg_owner[...], me)
    member = (iota((n, seg), 0) == relative).astype(F32)
    block = min(seg, 256)
    before = (iota((block, block), 0) < iota((block, block), 1)).astype(F32).astype(BF16)
    ahead_count = jnp.zeros((n, 1), F32)
    ranks = []
    for start in range(0, seg, block):
        part = member[:, start : start + block]
        count = dot(part.astype(BF16), before) + ahead_count
        ranks.append(jnp.sum(count * part, axis=0, keepdims=True))
        ahead_count = ahead_count + jnp.sum(part, axis=1, keepdims=True)
    rank = jnp.concatenate(ranks, axis=1).astype(jnp.int32)
    rank_ref[...] = (iota((cap, seg), 0) == rank).astype(F32).astype(BF16)
    memb_ref[...] = (iota((n * 8, seg), 0) // 8 == relative).astype(F32)
    cell = seg_cell[...]
    cell_row = (cell // nz).astype(F32)
    cell_z = (cell % nz).astype(F32)
    load("efield").wait()
    load("chain_start").wait()
    load("voltage").wait()

    link_behind = 1.0 - chain_start[...].astype(F32)
    eye = iota((cond, v_edge.shape[-1]), 0) == iota((cond, v_edge.shape[-1]), 1)
    seg_lane = iota((1, seg), 1)

    def pack_edge(column):
        row = jnp.sum(jnp.where(eye, column, 0.0), axis=0, keepdims=True)
        return jnp.broadcast_to(row, (8, row.shape[1]))

    def unpack_edge(block):
        return jnp.sum(jnp.where(eye, block[0:1], 0.0), axis=1, keepdims=True)

    def times(matrix, x):
        mh, ml = split(matrix)
        xh, xl = split(x)
        return dot(mh, xh) + dot(mh, xl) + dot(ml, xh)

    def to_slots(values):
        product = jnp.concatenate([values] * n, axis=0) * memb_ref[...]
        high, low = split(product)
        result = dot_nt(high, rank_ref[...]) + dot_nt(low, rank_ref[...])
        return result.reshape(n, 8, cap)

    def from_slots(block):
        high, low = split(block.reshape(n * 8, cap))
        spread = dot(high, rank_ref[...]) + dot(low, rank_ref[...])
        return jnp.sum((spread * memb_ref[...]).reshape(n, 8, seg), axis=0)

    def as_rows(index):
        return jnp.concatenate([msg_in[index, k] for k in range(n)], axis=1)

    def send_volt(volt, step):
        v_out[step] = pack_edge(volt[:, 0:1] * link_behind[:, 0:1])

        @pl.when(not_first)
        def _():
            v_copy(step).start()

    def pending_current(current, volt, step):
        @pl.when(not_last)
        def _():
            v_copy(step).wait_recv()

        edge = unpack_edge(v_edge[step])
        ahead = pltpu.roll(volt * link_behind, seg - 1, 1)
        ahead = jnp.where(seg_lane == seg - 1, edge, ahead)
        pending = current - times(induct[...], ahead - volt)
        j_ref[...] = pending
        values = [jnp.sum(couple[c] * pending, axis=0, keepdims=True) for c in range(3)]
        zeros = jnp.zeros((1, seg), F32)
        bout_ref[...] = to_slots(jnp.concatenate([zeros] * 3 + values + [zeros] * 2, axis=0))

    row_of = iota((rows, 1), 0)
    y_of = row_of % ny
    z_of = iota((1, nz), 1)

    def ahead_y(x):
        return jnp.where(y_of == ny - 1, 0.0, pltpu.roll(x, rows - 1, 0))

    def ahead_z(x):
        return jnp.where(z_of == nz - 1, 0.0, pltpu.roll(x, nz - 1, 1))

    def behind_y(x):
        return jnp.where(y_of == 0, 0.0, pltpu.roll(x, 1, 0))

    def behind_z(x):
        return jnp.where(z_of == 0, 0.0, pltpu.roll(x, 1, 1))

    def magnetic(efield, hfield, step):
        @pl.when(not_last)
        def _():
            e_copy(step).wait_recv()

        if step > 0:

            @pl.when(not_last)
            def _():
                h_copy(step - 1).wait_send()

        ex, ey, ez = efield[0], efield[1], efield[2]
        next_y = jnp.concatenate([ey[ny:], e_halo[step, 0]], axis=0)
        next_z = jnp.concatenate([ez[ny:], e_halo[step, 1]], axis=0)
        h_ref[1] = hfield[1] - COURANT * ((ahead_z(ex) - ex) - (next_z - ez))
        h_ref[2] = hfield[2] - COURANT * ((next_y - ey) - (ahead_y(ex) - ex))

        @pl.when(not_last)
        def _():
            h_copy(step).start()

        h_ref[0] = hfield[0] - COURANT * ((ahead_y(ez) - ez) - (ahead_z(ey) - ey))

    def electric(efield, density, step):
        @pl.when(not_first)
        def _():
            h_copy(step).wait_recv()
            e_copy(step).wait_send()

        hx, hy, hz = h_ref[0], h_ref[1], h_ref[2]
        prev_y = jnp.concatenate([h_halo[step, 0], hy[: rows - ny]], axis=0)
        prev_z = jnp.concatenate([h_halo[step, 1], hz[: rows - ny]], axis=0)
        keep, drive = keep_ref[...], drive_ref[...]
        ex, ey, ez = efield[0], efield[1], efield[2]
        curl_y = (hx - behind_z(hx)) - (hz - prev_z)
        e_ref[1] = keep * ey + drive * (curl_y - density[1])
        curl_z = (hy - prev_y) - (hx - behind_y(hx))
        e_ref[2] = keep * ez + drive * (curl_z - density[2])
        if step + 1 < STEPS:

            @pl.when(not_first)
            def _():
                e_copy(step + 1).start()

        curl_x = (hz - behind_y(hz)) - (hy - behind_z(hy))
        e_ref[0] = keep * ex + drive * (curl_x - density[0])

    chunk = 512

    def gather_cells(efield):
        high, low = split(efield.reshape(3 * rows, nz))
        for start in range(0, slots, chunk):
            part = pl.ds(start, chunk)
            onehot = ohz_ref[:, part]
            picked = dot(high, onehot) + dot(low, onehot)
            mask = ohr_ref[:, part].astype(F32)
            for c in range(3):
                eg_ref[c : c + 1, part] = jnp.sum(
                    picked[c * rows : (c + 1) * rows] * mask, axis=0, keepdims=True
                )

    def scatter_density(index):
        b = as_rows(index)
        e = [eg_ref[c : c + 1, :] for c in range(3)]
        m = [m_ref[i : i + 1, :] for i in range(6)]
        values = (
            b[3:4] + m[0] * e[0] + m[1] * e[1] + m[2] * e[2],
            b[4:5] + m[1] * e[0] + m[3] * e[1] + m[4] * e[2],
            b[5:6] + m[2] * e[0] + m[4] * e[1] + m[5] * e[2],
        )
        for c in range(3):
            high = values[c].astype(BF16).astype(F32)
            for i, value in enumerate((high, values[c] - high)):
                tile = jnp.broadcast_to(value, (16, slots)).astype(BF16)
                place = (i * 3 + c) * rows
                spread_ref[place : place + rows, :] = ohr_ref[...] * jnp.concatenate(
                    [tile] * (rows // 16), axis=0
                )
        total = dot_nt(spread_ref[...], ohz_ref[...])
        total = total[: 3 * rows] + total[3 * rows :]
        return [total[c * rows : (c + 1) * rows] for c in range(3)]

    def start_messages(step):
        for k in range(n):
            msg_out[2 + step, k] = bout_ref[k] + eg_ref[:, k * cap : (k + 1) * cap]
        send_messages(2 + step)

    msg_out[0] = to_slots(
        jnp.concatenate([cell_row, cell_z, jnp.zeros((6, seg), F32)], axis=0)
    )

    pl.semaphore_wait(barrier, n - 1)

    send_messages(0)

    @pl.when(not_first)
    def _():
        e_copy(0).start()

    send_volt(v_ref[...], 0)

    @pl.when(last)
    def _():
        e_halo[...] = jnp.zeros_like(e_halo)
        v_edge[...] = jnp.zeros_like(v_edge)

    @pl.when(first)
    def _():
        h_halo[...] = jnp.zeros_like(h_halo)
        i_edge[...] = jnp.zeros_like(i_edge)

    eg_ref[...] = jnp.zeros_like(eg_ref)

    load("induct").wait()
    load("couple").wait()
    for c in range(3):
        lc_ref[c] = times(induct[...], couple[c])
    quad = [jnp.sum(couple[a] * lc_ref[b], axis=0, keepdims=True) for a, b in PAIRS]
    msg_out[1] = to_slots(jnp.concatenate(quad + [jnp.zeros((2, seg), F32)], axis=0))
    send_messages(1)

    load("current").wait()
    pending_current(i_ref[...], v_ref[...], 0)

    for name in ("mat_eps", "mat_sigma", "material", "hfield", "capac"):
        load(name).wait()

    loss = mat_sigma[...] / (2.0 * mat_eps[...])
    keep_table = (1.0 - loss) / (1.0 + loss)
    drive_table = COURANT / (mat_eps[...] * (1.0 + loss))
    keep = jnp.zeros((rows, nz), F32)
    drive = jnp.zeros((rows, nz), F32)
    for i in range(mat_eps.shape[1]):
        here = material[...] == i
        keep = jnp.where(here, keep_table[:, i : i + 1], keep)
        drive = jnp.where(here, drive_table[:, i : i + 1], drive)
    keep_ref[...] = keep
    drive_ref[...] = drive

    wait_messages(0)
    cells = as_rows(0).astype(jnp.int32)
    ohr_ref[...] = (iota((rows, slots), 0) == cells[0:1]).astype(F32).astype(BF16)
    ohz_ref[...] = (iota((nz, slots), 0) == cells[1:2]).astype(F32).astype(BF16)

    gather_cells(e_ref[...])
    start_messages(0)
    magnetic(e_ref[...], h_ref[...], 0)
    wait_messages(1)
    m_ref[...] = as_rows(1)

    for step in range(STEPS):
        wait_messages(2 + step)
        seen = from_slots(msg_in[2 + step])
        current = (
            j_ref[...]
            + lc_ref[0] * seen[0:1]
            + lc_ref[1] * seen[1:2]
            + lc_ref[2] * seen[2:3]
        )
        i_ref[...] = current
        i_out[step] = pack_edge(current[:, seg - 1 : seg])

        @pl.when(not_last)
        def _():
            i_copy(step).start()

        density = scatter_density(2 + step)

        @pl.when(not_first)
        def _():
            i_copy(step).wait_recv()

        volt = v_ref[...]
        current = i_ref[...]
        edge = unpack_edge(i_edge[step])
        behind = jnp.where(seg_lane == 0, edge, pltpu.roll(current, 1, 1)) * link_behind
        volt = volt - times(capac[...], current - behind)
        v_ref[...] = volt
        if step + 1 < STEPS:
            send_volt(volt, step + 1)
        electric(e_ref[...], density, step)
        if step + 1 < STEPS:
            gather_cells(e_ref[...])
            pending_current(i_ref[...], v_ref[...], step + 1)
            start_messages(step + 1)
            magnetic(e_ref[...], h_ref[...], step + 1)

    for index in range(STEPS + 2):
        wait_sent(index)

    @pl.when(not_last)
    def _():
        h_copy(STEPS - 1).wait_send()
        for step in range(STEPS):
            i_copy(step).wait_send()

    @pl.when(not_first)
    def _():
        for step in range(STEPS):
            v_copy(step).wait_send()


def write_out(*refs):
    copies = [pltpu.make_async_copy(refs[i], refs[4 + i], refs[8].at[i]) for i in range(4)]
    for copy in copies:
        copy.start()
    for copy in copies:
        copy.wait()


def per_device(
    n,
    efield,
    hfield,
    material,
    mat_eps,
    mat_sigma,
    seg_owner,
    seg_cell,
    chain_start,
    couple,
    voltage,
    current,
    induct_step,
    capac_step,
):
    _, nx, ny, nz = efield.shape
    rows = nx * ny
    cond, seg = voltage.shape
    cap = -(-(2 * seg // n) // LANES) * LANES
    edge = -(-cond // LANES) * LANES
    slots = n * cap
    dma = pltpu.SemaphoreType.DMA
    scratch = [
        pltpu.VMEM((rows, nz), jnp.int32),
        pltpu.VMEM((1, mat_eps.shape[0]), F32),
        pltpu.VMEM((1, mat_eps.shape[0]), F32),
        pltpu.VMEM((1, seg), jnp.int32),
        pltpu.VMEM((1, seg), jnp.int32),
        pltpu.VMEM((1, seg), jnp.int32),
        pltpu.VMEM((3, cond, seg), F32),
        pltpu.VMEM((cond, cond), F32),
        pltpu.VMEM((cond, cond), F32),
        dma((13,)),
        pltpu.VMEM((rows, nz), F32),
        pltpu.VMEM((rows, nz), F32),
        pltpu.VMEM((n * 8, seg), F32),
        pltpu.VMEM((cap, seg), BF16),
        pltpu.VMEM((3, cond, seg), F32),
        pltpu.VMEM((cond, seg), F32),
        pltpu.VMEM((nz, slots), BF16),
        pltpu.VMEM((rows, slots), BF16),
        pltpu.VMEM((6 * rows, slots), BF16),
        pltpu.VMEM((8, slots), F32),
        pltpu.VMEM((8, slots), F32),
        pltpu.VMEM((n, 8, cap), F32),
        pltpu.VMEM((STEPS + 2, n, 8, cap), F32),
        pltpu.VMEM((STEPS + 2, n, 8, cap), F32),
        pltpu.VMEM((STEPS, 2, ny, nz), F32),
        pltpu.VMEM((STEPS, 2, ny, nz), F32),
        pltpu.VMEM((STEPS, 8, edge), F32),
        pltpu.VMEM((STEPS, 8, edge), F32),
        pltpu.VMEM((STEPS, 8, edge), F32),
        pltpu.VMEM((STEPS, 8, edge), F32),
        dma((STEPS + 2,)),
        dma((STEPS + 2,)),
    ] + [dma((STEPS,))] * 8
    vmem = pl.BlockSpec(memory_space=pltpu.VMEM)
    hbm = pl.BlockSpec(memory_space=pltpu.HBM)
    out = pl.pallas_call(
        functools.partial(kernel, n, ny),
        out_shape=(
            jax.ShapeDtypeStruct((3, rows, nz), F32),
            jax.ShapeDtypeStruct((3, rows, nz), F32),
            jax.ShapeDtypeStruct((cond, seg), F32),
            jax.ShapeDtypeStruct((cond, seg), F32),
        ),
        in_specs=[hbm] * 13,
        out_specs=(vmem,) * 4,
        scratch_shapes=scratch,
        compiler_params=pltpu.CompilerParams(
            collective_id=0, has_side_effects=True, vmem_limit_bytes=56 * 1024 * 1024
        ),
        name="leapfrog",
    )(
        efield.reshape(3, rows, nz),
        hfield.reshape(3, rows, nz),
        material.reshape(rows, nz),
        mat_eps.reshape(1, -1),
        mat_sigma.reshape(1, -1),
        seg_owner.reshape(1, seg),
        seg_cell.reshape(1, seg),
        chain_start.reshape(1, seg),
        couple,
        voltage,
        current,
        induct_step,
        capac_step,
    )
    out = pl.pallas_call(
        write_out,
        out_shape=tuple(jax.ShapeDtypeStruct(x.shape, x.dtype) for x in out),
        in_specs=[hbm] * 4,
        out_specs=(hbm,) * 4,
        scratch_shapes=[dma((4,))],
        compiler_params=pltpu.CompilerParams(vmem_limit_bytes=56 * 1024 * 1024),
        name="write_out",
    )(*out)
    return (
        out[0].reshape(efield.shape),
        out[1].reshape(hfield.shape),
        out[2],
        out[3],
    )


def solution(mesh):
    placed = (
        P(None, ("groups", "gx"), None, None),
        P(None, ("groups", "gx"), None, None),
        P(("groups", "gx"), None, None),
        P(),
        P(),
        P(("groups", "gx"), None),
        P(("groups", "gx")),
        P(("groups", "gx")),
        P(None, None, ("groups", "gx")),
        P(None, ("groups", "gx")),
        P(None, ("groups", "gx")),
        P(),
        P(),
    )
    return jax.shard_map(
        functools.partial(per_device, mesh.shape["gx"]),
        mesh=mesh,
        in_specs=placed,
        out_specs=(
            P(None, ("groups", "gx"), None, None),
            P(None, ("groups", "gx"), None, None),
            P(None, ("groups", "gx")),
            P(None, ("groups", "gx")),
        ),
        check_vma=False,
    )
```

```python
import functools

import jax
import jax.numpy as jnp
from jax import lax
from jax.experimental import pallas as pl
from jax.experimental.pallas import tpu as pltpu
from jax.sharding import PartitionSpec as P

STEPS = 4
COURANT = 0.55
MESH = pl.DeviceIdType.MESH
F32 = jnp.float32
BF16 = jnp.bfloat16
PAIRS = ((0, 0), (0, 1), (0, 2), (1, 1), (1, 2), (2, 2))
LANES = 128


def split(x):
    high = x.astype(BF16)
    return high, (x - high.astype(F32)).astype(BF16)


def dot(a, b):
    return jnp.dot(a, b, preferred_element_type=F32)


def dot_nt(a, b):
    return lax.dot_general(a, b, (((1,), (1,)), ((), ())), preferred_element_type=F32)


def iota(shape, dim):
    return lax.broadcasted_iota(jnp.int32, shape, dim)


def kernel(
    n,
    ny,
    *refs,
):
    sources, refs = refs[:13], refs[13:]
    (
        e_ref,
        h_ref,
        v_ref,
        i_ref,
        material,
        mat_eps,
        mat_sigma,
        seg_owner,
        seg_cell,
        chain_start,
        couple,
        induct,
        capac,
        load_sem,
        keep_ref,
        drive_ref,
        memb_ref,
        rank_ref,
        lc_ref,
        j_ref,
        ohz_ref,
        ohr_ref,
        spread_ref,
        m_ref,
        eg_ref,
        bout_ref,
        msg_out,
        msg_in,
        e_halo,
        h_halo,
        v_out,
        v_edge,
        i_out,
        i_edge,
        msg_ssem,
        msg_rsem,
        e_ssem,
        e_rsem,
        h_ssem,
        h_rsem,
        v_ssem,
        v_rsem,
        i_ssem,
        i_rsem,
    ) = refs
    me = lax.axis_index("gx")
    _, rows, nz = e_ref.shape
    cond, seg = v_ref.shape
    cap = msg_in.shape[-1]
    slots = n * cap
    first, last = me == 0, me == n - 1
    not_first, not_last = me > 0, me < n - 1

    def partner(k):
        result, bit = 0, 1
        while bit < n:
            digit = (me // bit) % 2
            result = result + (((1 - digit) if (k & bit) else digit) * bit)
            bit *= 2
        return result

    partners = [partner(k) for k in range(n)]

    places = {
        "seg_owner": (5, seg_owner),
        "seg_cell": (6, seg_cell),
        "efield": (0, e_ref),
        "chain_start": (7, chain_start),
        "voltage": (9, v_ref),
        "induct": (11, induct),
        "couple": (8, couple),
        "current": (10, i_ref),
        "mat_eps": (3, mat_eps),
        "mat_sigma": (4, mat_sigma),
        "material": (2, material),
        "hfield": (1, h_ref),
        "capac": (12, capac),
    }

    def load(name):
        index, target = places[name]
        return pltpu.make_async_copy(sources[index], target, load_sem.at[index])

    for name in places:
        load(name).start()

    barrier = pltpu.get_barrier_semaphore()
    for k in range(1, n):
        pl.semaphore_signal(barrier, inc=1, device_id={"gx": partners[k]}, device_id_type=MESH)

    def to_partner(index, k):
        return pltpu.make_async_remote_copy(
            src_ref=msg_out.at[index, k],
            dst_ref=msg_in.at[index, k],
            send_sem=msg_ssem.at[index],
            recv_sem=msg_rsem.at[index],
            device_id={"gx": partners[k]},
            device_id_type=MESH,
        )

    def send_messages(index):
        for k in range(1, n):
            to_partner(index, k).start()
        msg_in[index, 0] = msg_out[index, 0]

    def wait_messages(index):
        part = msg_in.at[index, pl.ds(1, n - 1)]
        pltpu.make_async_copy(part, part, msg_rsem.at[index]).wait()

    def wait_sent(index):
        part = msg_out.at[index, pl.ds(1, n - 1)]
        pltpu.make_async_copy(part, part, msg_ssem.at[index]).wait()

    def to_neighbour(source, target, ssem, rsem, step, direction):
        return pltpu.make_async_remote_copy(
            src_ref=source,
            dst_ref=target.at[step],
            send_sem=ssem.at[step],
            recv_sem=rsem.at[step],
            device_id={"gx": (me + direction + n) % n},
            device_id_type=MESH,
        )

    def e_copy(step):
        return to_neighbour(
            e_ref.at[pl.ds(1, 2), pl.ds(0, ny)], e_halo, e_ssem, e_rsem, step, -1
        )

    def h_copy(step):
        return to_neighbour(
            h_ref.at[pl.ds(1, 2), pl.ds(rows - ny, ny)], h_halo, h_ssem, h_rsem, step, 1
        )

    def v_copy(step):
        return to_neighbour(v_out.at[step], v_edge, v_ssem, v_rsem, step, -1)

    def i_copy(step):
        return to_neighbour(i_out.at[step], i_edge, i_ssem, i_rsem, step, 1)

    load("seg_owner").wait()
    load("seg_cell").wait()
    relative = jnp.bitwise_xor(seg_owner[...], me)
    member = (iota((n, seg), 0) == relative).astype(F32)
    block = min(seg, 256)
    before = (iota((block, block), 0) < iota((block, block), 1)).astype(F32).astype(BF16)
    ahead_count = jnp.zeros((n, 1), F32)
    ranks = []
    for start in range(0, seg, block):
        part = member[:, start : start + block]
        count = dot(part.astype(BF16), before) + ahead_count
        ranks.append(jnp.sum(count * part, axis=0, keepdims=True))
        ahead_count = ahead_count + jnp.sum(part, axis=1, keepdims=True)
    rank = jnp.concatenate(ranks, axis=1).astype(jnp.int32)
    rank_ref[...] = (iota((cap, seg), 0) == rank).astype(F32).astype(BF16)
    memb_ref[...] = (iota((n * 8, seg), 0) // 8 == relative).astype(F32)
    cell = seg_cell[...]
    cell_row = (cell // nz).astype(F32)
    cell_z = (cell % nz).astype(F32)
    load("efield").wait()
    load("chain_start").wait()
    load("voltage").wait()

    link_behind = 1.0 - chain_start[...].astype(F32)
    eye = iota((cond, v_edge.shape[-1]), 0) == iota((cond, v_edge.shape[-1]), 1)
    seg_lane = iota((1, seg), 1)

    def pack_edge(column):
        row = jnp.sum(jnp.where(eye, column, 0.0), axis=0, keepdims=True)
        return jnp.broadcast_to(row, (8, row.shape[1]))

    def unpack_edge(block):
        return jnp.sum(jnp.where(eye, block[0:1], 0.0), axis=1, keepdims=True)

    def times(matrix, x):
        mh, ml = split(matrix)
        xh, xl = split(x)
        return dot(mh, xh) + dot(mh, xl) + dot(ml, xh)

    def to_slots(values):
        product = jnp.concatenate([values] * n, axis=0) * memb_ref[...]
        high, low = split(product)
        result = dot_nt(high, rank_ref[...]) + dot_nt(low, rank_ref[...])
        return result.reshape(n, 8, cap)

    def from_slots(block):
        high, low = split(block.reshape(n * 8, cap))
        spread = dot(high, rank_ref[...]) + dot(low, rank_ref[...])
        return jnp.sum((spread * memb_ref[...]).reshape(n, 8, seg), axis=0)

    def as_rows(index):
        return jnp.concatenate([msg_in[index, k] for k in range(n)], axis=1)

    def send_volt(volt, step):
        v_out[step] = pack_edge(volt[:, 0:1] * link_behind[:, 0:1])

        @pl.when(not_first)
        def _():
            v_copy(step).start()

    def pending_current(current, volt, step):
        @pl.when(not_last)
        def _():
            v_copy(step).wait_recv()

        edge = unpack_edge(v_edge[step])
        ahead = pltpu.roll(volt * link_behind, seg - 1, 1)
        ahead = jnp.where(seg_lane == seg - 1, edge, ahead)
        pending = current - times(induct[...], ahead - volt)
        j_ref[...] = pending
        values = [jnp.sum(couple[c] * pending, axis=0, keepdims=True) for c in range(3)]
        zeros = jnp.zeros((1, seg), F32)
        bout_ref[...] = to_slots(jnp.concatenate([zeros] * 3 + values + [zeros] * 2, axis=0))

    row_of = iota((rows, 1), 0)
    y_of = row_of % ny
    z_of = iota((1, nz), 1)

    def ahead_y(x):
        return jnp.where(y_of == ny - 1, 0.0, pltpu.roll(x, rows - 1, 0))

    def ahead_z(x):
        return jnp.where(z_of == nz - 1, 0.0, pltpu.roll(x, nz - 1, 1))

    def behind_y(x):
        return jnp.where(y_of == 0, 0.0, pltpu.roll(x, 1, 0))

    def behind_z(x):
        return jnp.where(z_of == 0, 0.0, pltpu.roll(x, 1, 1))

    def magnetic(efield, hfield, step):
        @pl.when(not_last)
        def _():
            e_copy(step).wait_recv()

        if step > 0:

            @pl.when(not_last)
            def _():
                h_copy(step - 1).wait_send()

        ex, ey, ez = efield[0], efield[1], efield[2]
        next_y = jnp.concatenate([ey[ny:], e_halo[step, 0]], axis=0)
        next_z = jnp.concatenate([ez[ny:], e_halo[step, 1]], axis=0)
        h_ref[1] = hfield[1] - COURANT * ((ahead_z(ex) - ex) - (next_z - ez))
        h_ref[2] = hfield[2] - COURANT * ((next_y - ey) - (ahead_y(ex) - ex))

        @pl.when(not_last)
        def _():
            h_copy(step).start()

        h_ref[0] = hfield[0] - COURANT * ((ahead_y(ez) - ez) - (ahead_z(ey) - ey))

    def electric(efield, density, step):
        @pl.when(not_first)
        def _():
            h_copy(step).wait_recv()
            e_copy(step).wait_send()

        hx, hy, hz = h_ref[0], h_ref[1], h_ref[2]
        prev_y = jnp.concatenate([h_halo[step, 0], hy[: rows - ny]], axis=0)
        prev_z = jnp.concatenate([h_halo[step, 1], hz[: rows - ny]], axis=0)
        keep, drive = keep_ref[...], drive_ref[...]
        ex, ey, ez = efield[0], efield[1], efield[2]
        curl_y = (hx - behind_z(hx)) - (hz - prev_z)
        e_ref[1] = keep * ey + drive * (curl_y - density[1])
        curl_z = (hy - prev_y) - (hx - behind_y(hx))
        e_ref[2] = keep * ez + drive * (curl_z - density[2])
        if step + 1 < STEPS:

            @pl.when(not_first)
            def _():
                e_copy(step + 1).start()

        curl_x = (hz - behind_y(hz)) - (hy - behind_z(hy))
        e_ref[0] = keep * ex + drive * (curl_x - density[0])

    chunk = 512

    def gather_cells(efield):
        high, low = split(efield.reshape(3 * rows, nz))
        for start in range(0, slots, chunk):
            part = pl.ds(start, chunk)
            onehot = ohz_ref[:, part]
            picked = dot(high, onehot) + dot(low, onehot)
            mask = ohr_ref[:, part].astype(F32)
            for c in range(3):
                eg_ref[c : c + 1, part] = jnp.sum(
                    picked[c * rows : (c + 1) * rows] * mask, axis=0, keepdims=True
                )

    def scatter_density(index):
        b = as_rows(index)
        e = [eg_ref[c : c + 1, :] for c in range(3)]
        m = [m_ref[i : i + 1, :] for i in range(6)]
        values = (
            b[3:4] + m[0] * e[0] + m[1] * e[1] + m[2] * e[2],
            b[4:5] + m[1] * e[0] + m[3] * e[1] + m[4] * e[2],
            b[5:6] + m[2] * e[0] + m[4] * e[1] + m[5] * e[2],
        )
        for c in range(3):
            high = values[c].astype(BF16).astype(F32)
            for i, value in enumerate((high, values[c] - high)):
                tile = jnp.broadcast_to(value, (16, slots)).astype(BF16)
                place = (i * 3 + c) * rows
                spread_ref[place : place + rows, :] = ohr_ref[...] * jnp.concatenate(
                    [tile] * (rows // 16), axis=0
                )
        total = dot_nt(spread_ref[...], ohz_ref[...])
        total = total[: 3 * rows] + total[3 * rows :]
        return [total[c * rows : (c + 1) * rows] for c in range(3)]

    def start_messages(step):
        for k in range(n):
            msg_out[2 + step, k] = bout_ref[k] + eg_ref[:, k * cap : (k + 1) * cap]
        send_messages(2 + step)

    msg_out[0] = to_slots(
        jnp.concatenate([cell_row, cell_z, jnp.zeros((6, seg), F32)], axis=0)
    )

    pl.semaphore_wait(barrier, n - 1)

    send_messages(0)

    @pl.when(not_first)
    def _():
        e_copy(0).start()

    send_volt(v_ref[...], 0)

    @pl.when(last)
    def _():
        e_halo[...] = jnp.zeros_like(e_halo)
        v_edge[...] = jnp.zeros_like(v_edge)

    @pl.when(first)
    def _():
        h_halo[...] = jnp.zeros_like(h_halo)
        i_edge[...] = jnp.zeros_like(i_edge)

    eg_ref[...] = jnp.zeros_like(eg_ref)

    load("induct").wait()
    load("couple").wait()
    for c in range(3):
        lc_ref[c] = times(induct[...], couple[c])
    quad = [jnp.sum(couple[a] * lc_ref[b], axis=0, keepdims=True) for a, b in PAIRS]
    msg_out[1] = to_slots(jnp.concatenate(quad + [jnp.zeros((2, seg), F32)], axis=0))
    send_messages(1)

    load("current").wait()
    pending_current(i_ref[...], v_ref[...], 0)

    for name in ("mat_eps", "mat_sigma", "material", "hfield", "capac"):
        load(name).wait()

    loss = mat_sigma[...] / (2.0 * mat_eps[...])
    keep_table = (1.0 - loss) / (1.0 + loss)
    drive_table = COURANT / (mat_eps[...] * (1.0 + loss))
    keep = jnp.zeros((rows, nz), F32)
    drive = jnp.zeros((rows, nz), F32)
    for i in range(mat_eps.shape[1]):
        here = material[...] == i
        keep = jnp.where(here, keep_table[:, i : i + 1], keep)
        drive = jnp.where(here, drive_table[:, i : i + 1], drive)
    keep_ref[...] = keep
    drive_ref[...] = drive

    wait_messages(0)
    cells = as_rows(0).astype(jnp.int32)
    ohr_ref[...] = (iota((rows, slots), 0) == cells[0:1]).astype(F32).astype(BF16)
    ohz_ref[...] = (iota((nz, slots), 0) == cells[1:2]).astype(F32).astype(BF16)

    gather_cells(e_ref[...])
    start_messages(0)
    magnetic(e_ref[...], h_ref[...], 0)
    wait_messages(1)
    m_ref[...] = as_rows(1)

    for step in range(STEPS):
        wait_messages(2 + step)
        seen = from_slots(msg_in[2 + step])
        current = (
            j_ref[...]
            + lc_ref[0] * seen[0:1]
            + lc_ref[1] * seen[1:2]
            + lc_ref[2] * seen[2:3]
        )
        i_ref[...] = current
        i_out[step] = pack_edge(current[:, seg - 1 : seg])

        @pl.when(not_last)
        def _():
            i_copy(step).start()

        density = scatter_density(2 + step)

        @pl.when(not_first)
        def _():
            i_copy(step).wait_recv()

        volt = v_ref[...]
        current = i_ref[...]
        edge = unpack_edge(i_edge[step])
        behind = jnp.where(seg_lane == 0, edge, pltpu.roll(current, 1, 1)) * link_behind
        volt = volt - times(capac[...], current - behind)
        v_ref[...] = volt
        if step + 1 < STEPS:
            send_volt(volt, step + 1)
        electric(e_ref[...], density, step)
        if step + 1 < STEPS:
            gather_cells(e_ref[...])
            pending_current(i_ref[...], v_ref[...], step + 1)
            start_messages(step + 1)
            magnetic(e_ref[...], h_ref[...], step + 1)

    for index in range(STEPS + 2):
        wait_sent(index)

    @pl.when(not_last)
    def _():
        h_copy(STEPS - 1).wait_send()
        for step in range(STEPS):
            i_copy(step).wait_send()

    @pl.when(not_first)
    def _():
        for step in range(STEPS):
            v_copy(step).wait_send()


def write_out(*refs):
    loads = [pltpu.make_async_copy(refs[i], refs[8 + i], refs[12].at[i]) for i in range(4)]
    stores = [pltpu.make_async_copy(refs[8 + i], refs[4 + i], refs[13].at[i]) for i in range(4)]
    for load in loads:
        load.start()
    for load, store in zip(loads, stores):
        load.wait()
        store.start()
    for store in stores:
        store.wait()


def per_device(
    n,
    efield,
    hfield,
    material,
    mat_eps,
    mat_sigma,
    seg_owner,
    seg_cell,
    chain_start,
    couple,
    voltage,
    current,
    induct_step,
    capac_step,
):
    _, nx, ny, nz = efield.shape
    rows = nx * ny
    cond, seg = voltage.shape
    cap = -(-(2 * seg // n) // LANES) * LANES
    edge = -(-cond // LANES) * LANES
    slots = n * cap
    dma = pltpu.SemaphoreType.DMA
    scratch = [
        pltpu.VMEM((rows, nz), jnp.int32),
        pltpu.VMEM((1, mat_eps.shape[0]), F32),
        pltpu.VMEM((1, mat_eps.shape[0]), F32),
        pltpu.VMEM((1, seg), jnp.int32),
        pltpu.VMEM((1, seg), jnp.int32),
        pltpu.VMEM((1, seg), jnp.int32),
        pltpu.VMEM((3, cond, seg), F32),
        pltpu.VMEM((cond, cond), F32),
        pltpu.VMEM((cond, cond), F32),
        dma((13,)),
        pltpu.VMEM((rows, nz), F32),
        pltpu.VMEM((rows, nz), F32),
        pltpu.VMEM((n * 8, seg), F32),
        pltpu.VMEM((cap, seg), BF16),
        pltpu.VMEM((3, cond, seg), F32),
        pltpu.VMEM((cond, seg), F32),
        pltpu.VMEM((nz, slots), BF16),
        pltpu.VMEM((rows, slots), BF16),
        pltpu.VMEM((6 * rows, slots), BF16),
        pltpu.VMEM((8, slots), F32),
        pltpu.VMEM((8, slots), F32),
        pltpu.VMEM((n, 8, cap), F32),
        pltpu.VMEM((STEPS + 2, n, 8, cap), F32),
        pltpu.VMEM((STEPS + 2, n, 8, cap), F32),
        pltpu.VMEM((STEPS, 2, ny, nz), F32),
        pltpu.VMEM((STEPS, 2, ny, nz), F32),
        pltpu.VMEM((STEPS, 8, edge), F32),
        pltpu.VMEM((STEPS, 8, edge), F32),
        pltpu.VMEM((STEPS, 8, edge), F32),
        pltpu.VMEM((STEPS, 8, edge), F32),
        dma((STEPS + 2,)),
        dma((STEPS + 2,)),
    ] + [dma((STEPS,))] * 8
    vmem = pl.BlockSpec(memory_space=pltpu.VMEM)
    hbm = pl.BlockSpec(memory_space=pltpu.HBM)
    out = pl.pallas_call(
        functools.partial(kernel, n, ny),
        out_shape=(
            jax.ShapeDtypeStruct((3, rows, nz), F32),
            jax.ShapeDtypeStruct((3, rows, nz), F32),
            jax.ShapeDtypeStruct((cond, seg), F32),
            jax.ShapeDtypeStruct((cond, seg), F32),
        ),
        in_specs=[hbm] * 13,
        out_specs=(vmem,) * 4,
        scratch_shapes=scratch,
        compiler_params=pltpu.CompilerParams(
            collective_id=0, has_side_effects=True, vmem_limit_bytes=56 * 1024 * 1024
        ),
        name="leapfrog",
    )(
        efield.reshape(3, rows, nz),
        hfield.reshape(3, rows, nz),
        material.reshape(rows, nz),
        mat_eps.reshape(1, -1),
        mat_sigma.reshape(1, -1),
        seg_owner.reshape(1, seg),
        seg_cell.reshape(1, seg),
        chain_start.reshape(1, seg),
        couple,
        voltage,
        current,
        induct_step,
        capac_step,
    )
    out = pl.pallas_call(
        write_out,
        out_shape=tuple(jax.ShapeDtypeStruct(x.shape, x.dtype) for x in out),
        in_specs=[hbm] * 4,
        out_specs=(hbm,) * 4,
        scratch_shapes=[pltpu.VMEM(x.shape, x.dtype) for x in out] + [dma((4,))] * 2,
        compiler_params=pltpu.CompilerParams(vmem_limit_bytes=56 * 1024 * 1024),
        name="write_out",
    )(*out)
    return (
        out[0].reshape(efield.shape),
        out[1].reshape(hfield.shape),
        out[2],
        out[3],
    )


def solution(mesh):
    placed = (
        P(None, ("groups", "gx"), None, None),
        P(None, ("groups", "gx"), None, None),
        P(("groups", "gx"), None, None),
        P(),
        P(),
        P(("groups", "gx"), None),
        P(("groups", "gx")),
        P(("groups", "gx")),
        P(None, None, ("groups", "gx")),
        P(None, ("groups", "gx")),
        P(None, ("groups", "gx")),
        P(),
        P(),
    )
    return jax.shard_map(
        functools.partial(per_device, mesh.shape["gx"]),
        mesh=mesh,
        in_specs=placed,
        out_specs=(
            P(None, ("groups", "gx"), None, None),
            P(None, ("groups", "gx"), None, None),
            P(None, ("groups", "gx")),
            P(None, ("groups", "gx")),
        ),
        check_vma=False,
    )
```
